512 devices in a mesh: seq: 256 (over y_lo, z, x, core), head: 2 (over y_hi).
Axes of the slice: x: 4, y: 4 (y_hi: 2, y_lo: 2; y = y_hi * 2 + y_lo), z: 16, core: 2. Of those that a mesh axis runs over, the one named last changes fastest.
Arguments:
- query: bfloat16 [65536, 16, 128], P('seq', 'head'), may hold values from -6 to 6
- keys: bfloat16 [65536, 16, 128], P('seq', 'head'), may hold values from -6 to 6
- values: bfloat16 [65536, 16, 128], P('seq', 'head'), may hold values from -6 to 6
- cotangent: bfloat16 [65536, 16, 128], P('seq', 'head'), may hold values from -6 to 6
- gain: float32 [16, 128], P('head'), may hold values from 0.1 to 1.9
Outputs:
- normed: bfloat16 [65536, 16, 128], P('seq', 'head')
- grad_query: bfloat16 [65536, 16, 128], P('seq', 'head')
- grad_keys: bfloat16 [65536, 16, 128], P('seq', 'head')
- grad_values: bfloat16 [65536, 16, 128], P('seq', 'head')
- grad_gain: float32 [16, 128], P('head')
The draws below stay inside these ranges and needn't reach their ends.
All inputs are finite; a program needn't handle non-finite values.
Results may differ from the reference program's by a relative error of at most 0.0095.
Values may be sent and summed in bfloat16 or wider, within the bound.
A program may use at most 64 MiB of HBM per device.

```python
import jax
import jax.numpy as jnp
from jax import lax

HEADS = 16
HEAD_DIM = 128
BLOCK = 64
COARSE = 2
LEVELS = 4
TOK_DEV = 256
TOKENS = 65536
N_SEQ = 256


def base_normal(key):
    drawn = jax.random.normal(key, (TOKENS, HEADS, HEAD_DIM), jnp.float32)
    return jnp.clip(drawn, -6.0, 6.0)


def draw_query(key, part):
    key = jax.random.fold_in(key, 11)
    drawn = base_normal(key)
    return drawn.astype(jnp.bfloat16)


def draw_keys(key, part):
    key = jax.random.fold_in(key, 23)
    drawn = base_normal(key)
    return drawn.astype(jnp.bfloat16)


def block_levels(key, dims, pieces, low, high):
    def one(dim, shards_of):
        steps = jax.random.uniform(jax.random.fold_in(jax.random.fold_in(key, 6), dim), (shards_of,), jnp.float32, low / len(pieces), high / len(pieces))
        return jnp.repeat(jnp.exp(steps), dims[dim] // shards_of).reshape((-1,) + (1,) * (len(dims) - dim - 1))

    level = one(*pieces[0])
    for cut in pieces[1:]:
        level = level * one(*cut)
    return level


def scatter_about(own_key, dims, scale, reach, pieces=(), kind=jnp.bfloat16):
    values = scale * jax.random.normal(own_key, dims, jnp.float32)
    if pieces:
        values = values * block_levels(own_key, dims, pieces, -0.22, 0.18)
    return jnp.clip(values, -reach, reach).astype(kind)


def setup_inputs(seed: int = 0) -> dict:
    arg_keys = jax.random.split(jax.random.key(seed), 6)
    return {
        "query": draw_query(jax.random.fold_in(arg_keys[5], 71), 0),
        "keys": draw_keys(jax.random.fold_in(arg_keys[5], 71), 0),
        "values": scatter_about(arg_keys[2], (TOKENS, HEADS, HEAD_DIM), 1.0, 6.0, ((0, 256), (1, 2))),
        "cotangent": scatter_about(arg_keys[3], (TOKENS, HEADS, HEAD_DIM), 1.0, 6.0, ((0, 256), (1, 2))),
        "gain": jnp.clip(1.0 + 0.18 * jax.random.normal(arg_keys[4], (HEADS, HEAD_DIM), jnp.float32), 0.1, 1.9),
    }


EPSILON = 1e-05

def coarsen(tokens):
    groups = tokens.shape[0] // COARSE
    merged = tokens.astype(jnp.float32).reshape(groups, COARSE, tokens.shape[1], tokens.shape[2]).mean(axis=1)
    return merged.astype(jnp.bfloat16)

def shard_pass(query, keys, values, cotangent, near_keys, near_values, gain):
    row_count = query.shape[0]
    blocks = row_count // BLOCK
    score_scale = HEAD_DIM ** (-0.5)
    query_blocks = query.astype(jnp.float32).reshape(blocks, BLOCK, HEADS, HEAD_DIM)
    key_blocks = keys.astype(jnp.float32).reshape(blocks, BLOCK, HEADS, HEAD_DIM)
    value_blocks = values.astype(jnp.float32).reshape(blocks, BLOCK, HEADS, HEAD_DIM)
    far_keys = near_keys.astype(jnp.float32)
    far_values = near_values.astype(jnp.float32)
    local_scores = jnp.einsum('bqhe,bkhe->hbqk', query_blocks, key_blocks) * score_scale
    far_scores = jnp.einsum('bqhe,che->hbqc', query_blocks, far_keys) * score_scale
    row_max = jnp.maximum(local_scores.max(axis=-1), far_scores.max(axis=-1))
    local_exp = jnp.exp(local_scores - row_max[..., None])
    far_exp = jnp.exp(far_scores - row_max[..., None])
    denominator = local_exp.sum(axis=-1) + far_exp.sum(axis=-1)
    local_prob = local_exp / denominator[..., None]
    far_prob = far_exp / denominator[..., None]
    local_round = local_prob.astype(jnp.bfloat16).astype(jnp.float32)
    far_round = far_prob.astype(jnp.bfloat16).astype(jnp.float32)
    attention = jnp.einsum('hbqk,bkhe->bqhe', local_round, value_blocks) + jnp.einsum('hbqc,che->bqhe', far_round, far_values)
    attention = attention.reshape(row_count, HEADS, HEAD_DIM)
    squares = lax.optimization_barrier(jnp.sum(attention * attention, axis=(1, 2)))
    inverse = lax.rsqrt(squares / (HEADS * HEAD_DIM) + EPSILON)
    normed = (attention * inverse[:, None, None] * gain).astype(jnp.bfloat16)
    cotan_wide = cotangent.astype(jnp.float32)
    weighted = cotan_wide * gain
    slope = lax.optimization_barrier(jnp.sum(weighted * attention, axis=(1, 2)))
    grad_attention = weighted * inverse[:, None, None] - attention * (inverse ** 3 * slope / (HEADS * HEAD_DIM))[:, None, None]
    gain_terms = lax.optimization_barrier(jnp.sum(cotan_wide * attention * inverse[:, None, None], axis=0))
    grad_round = grad_attention.astype(jnp.bfloat16).astype(jnp.float32).reshape(blocks, BLOCK, HEADS, HEAD_DIM)
    local_grad_prob = jnp.einsum('bqhe,bkhe->hbqk', grad_round, value_blocks)
    far_grad_prob = jnp.einsum('bqhe,che->hbqc', grad_round, far_values)
    values_local = jnp.einsum('hbqk,bqhe->bkhe', local_round, grad_round)
    far_values_grad = jnp.einsum('hbqc,bqhe->che', far_round, grad_round)
    correction = (local_grad_prob * local_prob).sum(axis=-1) + (far_grad_prob * far_prob).sum(axis=-1)
    local_grad_scores = (local_prob * (local_grad_prob - correction[..., None]) * score_scale).astype(jnp.bfloat16).astype(jnp.float32)
    far_grad_scores = (far_prob * (far_grad_prob - correction[..., None]) * score_scale).astype(jnp.bfloat16).astype(jnp.float32)
    grad_query = jnp.einsum('hbqk,bkhe->bqhe', local_grad_scores, key_blocks) + jnp.einsum('hbqc,che->bqhe', far_grad_scores, far_keys)
    keys_local = jnp.einsum('hbqk,bqhe->bkhe', local_grad_scores, query_blocks)
    far_keys_grad = jnp.einsum('hbqc,bqhe->che', far_grad_scores, query_blocks)
    grad_query = grad_query.reshape(row_count, HEADS, HEAD_DIM).astype(jnp.bfloat16)
    keys_local = keys_local.reshape(row_count, HEADS, HEAD_DIM)
    values_local = values_local.reshape(row_count, HEADS, HEAD_DIM)
    return (normed, grad_query, keys_local, values_local, far_keys_grad, far_values_grad, gain_terms)

def reference(query, keys, values, cotangent, gain):
    shard_shape = (N_SEQ, TOK_DEV, HEADS, HEAD_DIM)
    query_shards = query.reshape(shard_shape)
    key_shards = keys.reshape(shard_shape)
    value_shards = values.reshape(shard_shape)
    cotan_shards = cotangent.reshape(shard_shape)
    coarse_keys = jax.vmap(coarsen)(key_shards)
    coarse_values = jax.vmap(coarsen)(value_shards)
    groups = TOK_DEV // COARSE
    distances = [N_SEQ >> level_index + 1 for level_index in range(LEVELS)]

    def visit(carry, shard_index):
        accum_keys, accum_values, gain_total = carry
        partner_ids = [jnp.bitwise_xor(shard_index, jnp.int32(distance)) for distance in distances]
        near_keys = jnp.concatenate([coarse_keys[partner] for partner in partner_ids], axis=0)
        near_values = jnp.concatenate([coarse_values[partner] for partner in partner_ids], axis=0)
        results = shard_pass(query_shards[shard_index], key_shards[shard_index], value_shards[shard_index], cotan_shards[shard_index], near_keys, near_values, gain)
        normed, grad_query, keys_local, values_local, far_keys_grad, far_values_grad, gain_terms = results
        for level_index, partner in enumerate(partner_ids):
            accum_keys = accum_keys.at[partner].add(far_keys_grad[level_index * groups:(level_index + 1) * groups])
            accum_values = accum_values.at[partner].add(far_values_grad[level_index * groups:(level_index + 1) * groups])
        return ((accum_keys, accum_values, gain_total + gain_terms), (normed, grad_query, keys_local, values_local))
    start = (jnp.zeros((N_SEQ, groups, HEADS, HEAD_DIM), jnp.float32), jnp.zeros((N_SEQ, groups, HEADS, HEAD_DIM), jnp.float32), jnp.zeros((HEADS, HEAD_DIM), jnp.float32))
    final, stacked = lax.scan(visit, start, jnp.arange(N_SEQ, dtype=jnp.int32))
    accum_keys, accum_values, grad_gain = final
    normed, grad_query, keys_local, values_local = stacked
    grad_keys = keys_local + jnp.repeat(accum_keys, COARSE, axis=1) / COARSE
    grad_values = values_local + jnp.repeat(accum_values, COARSE, axis=1) / COARSE
    whole = (TOKENS, HEADS, HEAD_DIM)
    return (normed.reshape(whole), grad_query.reshape(whole), grad_keys.reshape(whole).astype(jnp.bfloat16), grad_values.reshape(whole).astype(jnp.bfloat16), grad_gain)
```

```python
import functools

import jax
import jax.numpy as jnp
from jax import lax
from jax.experimental import pallas as pl
from jax.experimental.pallas import tpu as pltpu
from jax.sharding import PartitionSpec as P

HEADS = 16
HEAD_DIM = 128
BLOCK = 64
COARSE = 2
LEVELS = 4
EPSILON = 1e-05
MESH = pl.DeviceIdType.MESH
NT = (((1,), (1,)), ((), ()))
TN = (((0,), (0,)), ((), ()))

F0, F1, F2, F3, B0, B1, B2, B3 = range(8)


def flipped(index, distance):
    return index + distance - 2 * distance * ((index // distance) % 2)


def dot(left, right, dims=(((1,), (0,)), ((), ()))):
    return lax.dot_general(left, right, dims, preferred_element_type=jnp.float32)


def kernel(
    n_seq, query_ref, keys_ref, values_ref, cotan_ref, gain_ref,
    normed_ref, gquery_ref, gkeys_ref, gvalues_ref, ggain_ref,
    q_rows, k_rows, v_rows, c_rows, ck_rows, cv_rows,
    own, far, probs, attn, sq_sum, slope_sum, norm_out, norm_in, inv_wide, coef_wide,
    grad_out, grad_in, level2, gain_out, gain_in,
    normed_rows, gq_rows, gk_rows, gv_rows,
    send_sem, recv_sem, norm_sems, gain_send, gain_recv,
):
    tokens, heads, width = query_ref.shape
    groups = tokens // COARSE
    scale = width ** (-0.5)
    me = lax.axis_index("seq")
    side = lax.axis_index("head")
    distances = [n_seq >> level + 1 for level in range(LEVELS)]
    at0, at2, at3 = (flipped(me, distances[level]) for level in (0, 2, 3))
    relay = flipped(at2, distances[1])
    low = []
    while 1 << len(low) < distances[3]:
        low.append(flipped(me, 1 << len(low)))
    ring = low + [at3, at2, relay, at0]

    barrier = pltpu.get_barrier_semaphore()
    for partner in ring:
        pl.semaphore_signal(barrier, inc=1, device_id={"seq": partner}, device_id_type=MESH)
    pl.semaphore_signal(barrier, inc=1, device_id={"head": 1 - side}, device_id_type=MESH)

    def transfer(kind, head):
        source, target, partner = {
            F0: (own, far.at[0], at0),
            F1: (far.at[2], far.at[1], relay),
            F2: (own, far.at[2], at2),
            F3: (own, far.at[3], at3),
            B0: (grad_out.at[0], grad_in.at[0], at0),
            B1: (grad_out.at[1], grad_in.at[1], relay),
            B2: (grad_out.at[2], grad_in.at[2], at2),
            B3: (grad_out.at[3], grad_in.at[3], at3),
        }[kind]
        return pltpu.make_async_remote_copy(
            src_ref=source.at[head],
            dst_ref=target.at[head],
            send_sem=send_sem.at[kind, head],
            recv_sem=recv_sem.at[kind, head],
            device_id={"seq": partner},
            device_id_type=MESH,
        )

    def loop(count, body):
        def run(step, carry):
            body(step)
            return carry

        lax.fori_loop(0, count, run, 0)

    slab = 16

    def spread(ref, rows):
        def body(step):
            part = ref[pl.ds(step * slab, slab)].astype(jnp.float32)
            rows[pl.ds(pl.multiple_of(step * slab * heads, 8), slab * heads), :] = part.reshape(
                slab * heads, width
            )

        loop(tokens // slab, body)

    def coarsen(ref, rows, coarse_rows):
        def body(step):
            part = ref[pl.ds(step * slab, slab)].astype(jnp.float32)
            rows[pl.ds(pl.multiple_of(step * slab * heads, 8), slab * heads), :] = part.reshape(
                slab * heads, width
            )
            pairs = part.reshape(slab // 2, 2, heads, width)
            mean = (pairs[:, 0] + pairs[:, 1]) * 0.5
            half = slab // 2 * heads
            coarse_rows[pl.ds(pl.multiple_of(step * half, 8), half), :] = mean.reshape(half, width)

        loop(tokens // slab, body)

    def pick(rows, head, count):
        return rows[pl.ds(head, count, stride=heads), :]

    coarsen(keys_ref, k_rows, ck_rows)
    coarsen(values_ref, v_rows, cv_rows)

    def pack(head):
        own[head, :groups, :] = pick(ck_rows, head, groups).astype(jnp.bfloat16)
        own[head, groups:, :] = pick(cv_rows, head, groups).astype(jnp.bfloat16)

    loop(heads, pack)
    pl.semaphore_wait(barrier, len(ring) + 1)

    def first(head):
        transfer(F2, head).start()
        transfer(F0, head).start()

    loop(heads, first)
    early = heads // 4
    loop(early, lambda head: transfer(F3, head).start())
    spread(query_ref, q_rows)
    spread(cotan_ref, c_rows)
    sq_sum[...] = jnp.zeros_like(sq_sum)
    slope_sum[...] = jnp.zeros_like(slope_sum)

    def forward(head):
        transfer(F2, head).wait_recv()
        transfer(F1, head).start()

        @pl.when(head >= early)
        def _():
            transfer(F3, head).start()

    loop(heads, forward)

    span = 2 * BLOCK
    row_block = lax.broadcasted_iota(jnp.int32, (span, span), 0) < BLOCK
    col_block = lax.broadcasted_iota(jnp.int32, (span, span), 1) < BLOCK
    inside = row_block == col_block
    spans = [slice(start, start + span) for start in range(0, tokens, span)]

    def attend(head):
        transfer(F0, head).wait_recv()
        transfer(F1, head).wait_recv()
        transfer(F3, head).wait_recv()
        query = pick(q_rows, head, tokens).astype(jnp.bfloat16)
        key = pick(k_rows, head, tokens).astype(jnp.bfloat16)
        value = pick(v_rows, head, tokens).astype(jnp.bfloat16)
        near = [
            jnp.where(inside, dot(query[part], key[part], NT) * scale, -1e30) for part in spans
        ]
        scores = [jnp.concatenate(near, axis=0)] + [
            dot(query, far[level, head, :groups, :], NT) * scale for level in range(LEVELS)
        ]
        scores = jnp.concatenate(scores, axis=1)
        top = jnp.max(scores, axis=1, keepdims=True)
        weights = jnp.exp(scores - top)
        total = jnp.sum(weights, axis=1, keepdims=True)
        prob = weights * (1.0 / total)
        probs[head] = prob
        rounded = prob.astype(jnp.bfloat16)
        out = jnp.concatenate([dot(rounded[part, :span], value[part]) for part in spans], axis=0)
        for level in range(LEVELS):
            start = span + level * groups
            out = out + dot(rounded[:, start : start + groups], far[level, head, groups:, :])
        attn[head] = out
        weighted = pick(c_rows, head, tokens) * gain_ref[pl.ds(head, 1), :]
        sq_sum[...] += out * out
        slope_sum[...] += weighted * out

    loop(heads, attend)

    norm_out[...] = jnp.zeros_like(norm_out)
    norm_out[0:1, :] = jnp.sum(sq_sum[...].T, axis=0, keepdims=True)
    norm_out[1:2, :] = jnp.sum(slope_sum[...].T, axis=0, keepdims=True)
    norm_copy = pltpu.make_async_remote_copy(
        src_ref=norm_out,
        dst_ref=norm_in,
        send_sem=norm_sems.at[0],
        recv_sem=norm_sems.at[1],
        device_id={"head": 1 - side},
        device_id_type=MESH,
    )
    norm_copy.start()
    norm_copy.wait()
    squares = norm_out[0:1, :] + norm_in[0:1, :]
    slope = norm_out[1:2, :] + norm_in[1:2, :]
    inverse = lax.rsqrt(squares / (HEADS * HEAD_DIM) + EPSILON)
    coef = inverse * inverse * inverse * slope / (HEADS * HEAD_DIM)
    inv_wide[...] = jnp.broadcast_to(inverse, (width, tokens)).T
    coef_wide[...] = jnp.broadcast_to(coef, (width, tokens)).T

    def join(head):
        transfer(B1, head).wait_recv()
        grad_out[2, head] = (level2[head] + grad_in[1, head].astype(jnp.float32)).astype(
            jnp.bfloat16
        )
        transfer(B2, head).start()

    def backward(head):
        query = pick(q_rows, head, tokens).astype(jnp.bfloat16)
        key = pick(k_rows, head, tokens).astype(jnp.bfloat16)
        value = pick(v_rows, head, tokens).astype(jnp.bfloat16)
        out = attn[head]
        gain = gain_ref[pl.ds(head, 1), :]
        cotan = pick(c_rows, head, tokens)
        direction = out * inv_wide[...]
        grad_attn = cotan * gain * inv_wide[...] - out * coef_wide[...]
        grad = grad_attn.astype(jnp.bfloat16)
        prob = probs[head]
        rounded = prob.astype(jnp.bfloat16)
        grad_prob = [
            jnp.concatenate([dot(grad[part], value[part], NT) for part in spans], axis=0)
        ] + [dot(grad, far[level, head, groups:, :], NT) for level in range(LEVELS)]
        grad_prob = jnp.concatenate(grad_prob, axis=1)
        correction = jnp.sum(grad_prob * prob, axis=1, keepdims=True)
        grad_score = (prob * (grad_prob - correction) * scale).astype(jnp.bfloat16)
        for level in (1, 0, 3, 2):
            start = span + level * groups
            dkey = dot(grad_score[:, start : start + groups], query, TN)
            dvalue = dot(rounded[:, start : start + groups], grad, TN)
            if level == 2:
                level2[head, :groups, :] = dkey
                level2[head, groups:, :] = dvalue
            else:
                grad_out[level, head, :groups, :] = dkey.astype(jnp.bfloat16)
                grad_out[level, head, groups:, :] = dvalue.astype(jnp.bfloat16)
            if level == 1:
                transfer(B1, head).start()
            elif level == 0:
                transfer(B0, head).start()
            elif level == 3:

                @pl.when(head < early)
                def _():
                    transfer(B3, head).start()

        gquery = jnp.concatenate([dot(grad_score[part, :span], key[part]) for part in spans], axis=0)
        for level in range(LEVELS):
            start = span + level * groups
            gquery = gquery + dot(grad_score[:, start : start + groups], far[level, head, :groups, :])
        here = pl.ds(head, tokens, stride=heads)
        gq_rows[here, :] = gquery
        gk_rows[here, :] = jnp.concatenate(
            [dot(grad_score[part, :span], query[part], TN) for part in spans], axis=0
        )
        gv_rows[here, :] = jnp.concatenate(
            [dot(rounded[part, :span], grad[part], TN) for part in spans], axis=0
        )
        normed_rows[here, :] = direction * gain
        gain_out[0, pl.ds(head, 1), :] = jnp.sum(cotan * direction, axis=0, keepdims=True)

        @pl.when(head >= early)
        def _():
            join(head - early)
            transfer(B3, head).start()

    loop(heads, backward)

    def gain_copy(step):
        return pltpu.make_async_remote_copy(
            src_ref=gain_out.at[step],
            dst_ref=gain_in.at[step],
            send_sem=gain_send.at[step],
            recv_sem=gain_recv.at[step],
            device_id={"seq": ring[step]},
            device_id_type=MESH,
        )

    def gain_step(step):
        if step:
            gain_copy(step - 1).wait_recv()
            gain_out[step] = gain_out[step - 1] + gain_in[step - 1]
        if step < len(ring):
            gain_copy(step).start()

    def gather(rows, ref):
        def body(step):
            part = rows[pl.ds(pl.multiple_of(step * slab * heads, 8), slab * heads), :]
            ref[pl.ds(step * slab, slab)] = part.reshape(slab, heads, width).astype(jnp.bfloat16)

        loop(tokens // slab, body)

    for step in range(early):
        gain_step(step)
        join(heads - early + step)
    gather(normed_rows, normed_ref)
    gather(gq_rows, gquery_ref)
    for step in range(early, len(ring) + 1):
        gain_step(step)
    ggain_ref[...] = gain_out[len(ring)]

    def collect(head):
        for kind in (B0, B2, B3):
            transfer(kind, head).wait_recv()
        total = (
            grad_in[0, head].astype(jnp.float32)
            + grad_in[2, head].astype(jnp.float32)
            + grad_in[3, head].astype(jnp.float32)
        )
        here = pl.ds(head, groups, stride=heads)
        ck_rows[here, :] = total[:groups] * (1.0 / COARSE)
        cv_rows[here, :] = total[groups:] * (1.0 / COARSE)

    loop(heads, collect)

    def merge(rows, coarse_rows, ref):
        def body(step):
            part = rows[pl.ds(pl.multiple_of(step * slab * heads, 8), slab * heads), :]
            half = slab // 2 * heads
            coarse = coarse_rows[pl.ds(pl.multiple_of(step * half, 8), half), :]
            whole = part.reshape(slab // 2, 2, heads, width) + coarse.reshape(
                slab // 2, 1, heads, width
            )
            ref[pl.ds(step * slab, slab)] = whole.reshape(slab, heads, width).astype(jnp.bfloat16)

        loop(tokens // slab, body)

    merge(gk_rows, ck_rows, gkeys_ref)
    merge(gv_rows, cv_rows, gvalues_ref)

    def drain(head):
        for kind in range(8):
            transfer(kind, head).wait_send()

    loop(heads, drain)
    for step in range(len(ring)):
        gain_copy(step).wait_send()


def local(n_seq, query, keys, values, cotangent, gain):
    tokens, heads, width = query.shape
    groups = tokens // COARSE
    steps = n_seq.bit_length() - 1
    columns = 2 * BLOCK + LEVELS * groups
    whole = jax.ShapeDtypeStruct(query.shape, jnp.bfloat16)
    vmem = pl.BlockSpec(memory_space=pltpu.VMEM)
    rows = pltpu.VMEM((tokens * heads, width), jnp.float32)
    coarse_rows = pltpu.VMEM((groups * heads, width), jnp.float32)
    wide = pltpu.VMEM((tokens, width), jnp.float32)
    pairs = (heads, 2 * groups, width)
    return pl.pallas_call(
        functools.partial(kernel, n_seq),
        out_shape=[whole] * 4 + [jax.ShapeDtypeStruct(gain.shape, jnp.float32)],
        in_specs=[vmem] * 5,
        out_specs=[vmem] * 5,
        scratch_shapes=[
            rows, rows, rows, rows, coarse_rows, coarse_rows,
            pltpu.VMEM(pairs, jnp.bfloat16),
            pltpu.VMEM((LEVELS,) + pairs, jnp.bfloat16),
            pltpu.VMEM((heads, tokens, columns), jnp.float32),
            pltpu.VMEM((heads, tokens, width), jnp.float32),
            wide, wide,
            pltpu.VMEM((8, tokens), jnp.float32),
            pltpu.VMEM((8, tokens), jnp.float32),
            wide, wide,
            pltpu.VMEM((LEVELS,) + pairs, jnp.bfloat16),
            pltpu.VMEM((LEVELS,) + pairs, jnp.bfloat16),
            pltpu.VMEM(pairs, jnp.float32),
            pltpu.VMEM((steps + 1,) + gain.shape, jnp.float32),
            pltpu.VMEM((steps,) + gain.shape, jnp.float32),
            rows, rows, rows, rows,
            pltpu.SemaphoreType.DMA((8, heads)),
            pltpu.SemaphoreType.DMA((8, heads)),
            pltpu.SemaphoreType.DMA((2,)),
            pltpu.SemaphoreType.DMA((steps,)),
            pltpu.SemaphoreType.DMA((steps,)),
        ],
        compiler_params=pltpu.CompilerParams(
            collective_id=0, has_side_effects=True, vmem_limit_bytes=48 * 2**20
        ),
        cost_estimate=pl.CostEstimate(
            flops=1_800_000_000, bytes_accessed=4 * 2**20, transcendentals=1_200_000
        ),
    )(query, keys, values, cotangent, gain)


def solution(mesh):
    spec = P("seq", "head", None)
    return jax.shard_map(
        functools.partial(local, mesh.shape["seq"]),
        mesh=mesh,
        in_specs=(spec, spec, spec, spec, P("head", None)),
        out_specs=(spec, spec, spec, spec, P("head", None)),
        check_vma=False,
    )
```

```python
import functools

import jax
import jax.numpy as jnp
from jax import lax
from jax.experimental import pallas as pl
from jax.experimental.pallas import tpu as pltpu
from jax.sharding import PartitionSpec as P

HEADS = 16
HEAD_DIM = 128
BLOCK = 64
COARSE = 2
LEVELS = 4
EPSILON = 1e-05
MESH = pl.DeviceIdType.MESH
NT = (((1,), (1,)), ((), ()))
TN = (((0,), (0,)), ((), ()))

F0, F1, F2, F3, B0, B1, B2, B3 = range(8)


def flipped(index, distance):
    return index + distance - 2 * distance * ((index // distance) % 2)


def dot(left, right, dims=(((1,), (0,)), ((), ()))):
    return lax.dot_general(left, right, dims, preferred_element_type=jnp.float32)


def kernel(
    n_seq, query_hbm, keys_hbm, values_hbm, cotan_hbm, gain_hbm,
    normed_ref, gquery_ref, gkeys_ref, gvalues_ref, ggain_ref,
    query_ref, keys_ref, values_ref, cotan_ref, gain_ref, load_sems,
    q_rows, k_rows, v_rows, c_rows, ck_rows, cv_rows,
    own, far, probs, attn, sq_sum, slope_sum, norm_out, norm_in, inv_wide, coef_wide,
    grad_out, grad_in, level2, gain_out, gain_in,
    normed_rows, gq_rows, gk_rows, gv_rows,
    send_sem, recv_sem, norm_sems, gain_send, gain_recv,
):
    loads = [
        pltpu.make_async_copy(source, target, load_sems.at[number])
        for number, (source, target) in enumerate(
            [
                (keys_hbm, keys_ref),
                (values_hbm, values_ref),
                (query_hbm, query_ref),
                (cotan_hbm, cotan_ref),
                (gain_hbm, gain_ref),
            ]
        )
    ]
    for load in loads:
        load.start()
    tokens, heads, width = query_ref.shape
    groups = tokens // COARSE
    scale = width ** (-0.5)
    me = lax.axis_index("seq")
    side = lax.axis_index("head")
    distances = [n_seq >> level + 1 for level in range(LEVELS)]
    at0, at2, at3 = (flipped(me, distances[level]) for level in (0, 2, 3))
    relay = flipped(at2, distances[1])
    low = []
    while 1 << len(low) < distances[3]:
        low.append(flipped(me, 1 << len(low)))
    ring = low + [at3, at2, relay, at0]

    barrier = pltpu.get_barrier_semaphore()
    for partner in ring:
        pl.semaphore_signal(barrier, inc=1, device_id={"seq": partner}, device_id_type=MESH)
    pl.semaphore_signal(barrier, inc=1, device_id={"head": 1 - side}, device_id_type=MESH)

    def transfer(kind, head):
        source, target, partner = {
            F0: (own, far.at[0], at0),
            F1: (far.at[2], far.at[1], relay),
            F2: (own, far.at[2], at2),
            F3: (own, far.at[3], at3),
            B0: (grad_out.at[0], grad_in.at[0], at0),
            B1: (grad_out.at[1], grad_in.at[1], relay),
            B2: (grad_out.at[2], grad_in.at[2], at2),
            B3: (grad_out.at[3], grad_in.at[3], at3),
        }[kind]
        return pltpu.make_async_remote_copy(
            src_ref=source.at[head],
            dst_ref=target.at[head],
            send_sem=send_sem.at[kind, head],
            recv_sem=recv_sem.at[kind, head],
            device_id={"seq": partner},
            device_id_type=MESH,
        )

    def loop(count, body):
        def run(step, carry):
            body(step)
            return carry

        lax.fori_loop(0, count, run, 0)

    slab = 16

    def spread(ref, rows):
        def body(step):
            part = ref[pl.ds(step * slab, slab)].astype(jnp.float32)
            rows[pl.ds(pl.multiple_of(step * slab * heads, 8), slab * heads), :] = part.reshape(
                slab * heads, width
            )

        loop(tokens // slab, body)

    def coarsen(ref, rows, coarse_rows):
        def body(step):
            part = ref[pl.ds(step * slab, slab)].astype(jnp.float32)
            rows[pl.ds(pl.multiple_of(step * slab * heads, 8), slab * heads), :] = part.reshape(
                slab * heads, width
            )
            pairs = part.reshape(slab // 2, 2, heads, width)
            mean = (pairs[:, 0] + pairs[:, 1]) * 0.5
            half = slab // 2 * heads
            coarse_rows[pl.ds(pl.multiple_of(step * half, 8), half), :] = mean.reshape(half, width)

        loop(tokens // slab, body)

    def pick(rows, head, count):
        return rows[pl.ds(head, count, stride=heads), :]

    loads[0].wait()
    coarsen(keys_ref, k_rows, ck_rows)
    loads[1].wait()
    coarsen(values_ref, v_rows, cv_rows)

    def pack(head):
        own[head, :groups, :] = pick(ck_rows, head, groups).astype(jnp.bfloat16)
        own[head, groups:, :] = pick(cv_rows, head, groups).astype(jnp.bfloat16)

    loop(heads, pack)
    pl.semaphore_wait(barrier, len(ring) + 1)

    def first(head):
        transfer(F2, head).start()
        transfer(F0, head).start()

    loop(heads, first)
    early = heads // 2
    loop(early, lambda head: transfer(F3, head).start())
    for load in loads[2:]:
        load.wait()
    spread(query_ref, q_rows)
    spread(cotan_ref, c_rows)
    sq_sum[...] = jnp.zeros_like(sq_sum)
    slope_sum[...] = jnp.zeros_like(slope_sum)

    def forward(head):
        transfer(F2, head).wait_recv()
        transfer(F1, head).start()

        @pl.when(head >= early)
        def _():
            transfer(F3, head).start()

    loop(heads, forward)

    span = 2 * BLOCK
    row_block = lax.broadcasted_iota(jnp.int32, (span, span), 0) < BLOCK
    col_block = lax.broadcasted_iota(jnp.int32, (span, span), 1) < BLOCK
    inside = row_block == col_block
    spans = [slice(start, start + span) for start in range(0, tokens, span)]

    def attend(head):
        transfer(F0, head).wait_recv()
        transfer(F1, head).wait_recv()
        transfer(F3, head).wait_recv()
        query = pick(q_rows, head, tokens).astype(jnp.bfloat16)
        key = pick(k_rows, head, tokens).astype(jnp.bfloat16)
        value = pick(v_rows, head, tokens).astype(jnp.bfloat16)
        near = [
            jnp.where(inside, dot(query[part], key[part], NT) * scale, -1e30) for part in spans
        ]
        scores = [jnp.concatenate(near, axis=0)] + [
            dot(query, far[level, head, :groups, :], NT) * scale for level in range(LEVELS)
        ]
        scores = jnp.concatenate(scores, axis=1)
        top = jnp.max(scores, axis=1, keepdims=True)
        weights = jnp.exp(scores - top)
        total = jnp.sum(weights, axis=1, keepdims=True)
        prob = weights * (1.0 / total)
        probs[head] = prob
        rounded = prob.astype(jnp.bfloat16)
        out = jnp.concatenate([dot(rounded[part, :span], value[part]) for part in spans], axis=0)
        for level in range(LEVELS):
            start = span + level * groups
            out = out + dot(rounded[:, start : start + groups], far[level, head, groups:, :])
        attn[head] = out
        weighted = pick(c_rows, head, tokens) * gain_ref[pl.ds(head, 1), :]
        sq_sum[...] += out * out
        slope_sum[...] += weighted * out

    loop(heads, attend)

    norm_out[...] = jnp.zeros_like(norm_out)
    norm_out[0:1, :] = jnp.sum(sq_sum[...].T, axis=0, keepdims=True)
    norm_out[1:2, :] = jnp.sum(slope_sum[...].T, axis=0, keepdims=True)
    norm_copy = pltpu.make_async_remote_copy(
        src_ref=norm_out,
        dst_ref=norm_in,
        send_sem=norm_sems.at[0],
        recv_sem=norm_sems.at[1],
        device_id={"head": 1 - side},
        device_id_type=MESH,
    )
    norm_copy.start()
    norm_copy.wait()
    squares = norm_out[0:1, :] + norm_in[0:1, :]
    slope = norm_out[1:2, :] + norm_in[1:2, :]
    inverse = lax.rsqrt(squares / (HEADS * HEAD_DIM) + EPSILON)
    coef = inverse * inverse * inverse * slope / (HEADS * HEAD_DIM)
    inv_wide[...] = jnp.broadcast_to(inverse, (width, tokens)).T
    coef_wide[...] = jnp.broadcast_to(coef, (width, tokens)).T

    def join(head):
        transfer(B1, head).wait_recv()
        grad_out[2, head] = (level2[head] + grad_in[1, head].astype(jnp.float32)).astype(
            jnp.bfloat16
        )
        transfer(B2, head).start()

    lag = 3
    gain_ring = [ring[3], at3, at2, relay] + ring[:3] + [at0]

    def gain_terms(head):
        direction = attn[head] * inv_wide[...]
        gain_out[0, pl.ds(head, 1), :] = jnp.sum(
            pick(c_rows, head, tokens) * direction, axis=0, keepdims=True
        )

    def gain_copy(step):
        return pltpu.make_async_remote_copy(
            src_ref=gain_out.at[step],
            dst_ref=gain_in.at[step],
            send_sem=gain_send.at[step],
            recv_sem=gain_recv.at[step],
            device_id={"seq": gain_ring[step]},
            device_id_type=MESH,
        )

    def gain_step(step):
        if step:
            gain_copy(step - 1).wait_recv()
            gain_out[step] = gain_out[step - 1] + gain_in[step - 1]
        if step < len(gain_ring):
            gain_copy(step).start()

    def backward(head):
        query = pick(q_rows, head, tokens).astype(jnp.bfloat16)
        key = pick(k_rows, head, tokens).astype(jnp.bfloat16)
        value = pick(v_rows, head, tokens).astype(jnp.bfloat16)
        out = attn[head]
        gain = gain_ref[pl.ds(head, 1), :]
        cotan = pick(c_rows, head, tokens)
        direction = out * inv_wide[...]
        grad_attn = cotan * gain * inv_wide[...] - out * coef_wide[...]
        grad = grad_attn.astype(jnp.bfloat16)
        prob = probs[head]
        rounded = prob.astype(jnp.bfloat16)
        grad_prob = [
            jnp.concatenate([dot(grad[part], value[part], NT) for part in spans], axis=0)
        ] + [dot(grad, far[level, head, groups:, :], NT) for level in range(LEVELS)]
        grad_prob = jnp.concatenate(grad_prob, axis=1)
        correction = jnp.sum(grad_prob * prob, axis=1, keepdims=True)
        grad_score = (prob * (grad_prob - correction) * scale).astype(jnp.bfloat16)
        for level in (1, 0, 3, 2):
            start = span + level * groups
            dkey = dot(grad_score[:, start : start + groups], query, TN)
            dvalue = dot(rounded[:, start : start + groups], grad, TN)
            if level == 2:
                level2[head, :groups, :] = dkey
                level2[head, groups:, :] = dvalue
            else:
                grad_out[level, head, :groups, :] = dkey.astype(jnp.bfloat16)
                grad_out[level, head, groups:, :] = dvalue.astype(jnp.bfloat16)
            if level == 1:
                transfer(B1, head).start()
            elif level == 0:
                transfer(B0, head).start()
            elif level == 3:
                transfer(B3, head).start()

        gquery = jnp.concatenate([dot(grad_score[part, :span], key[part]) for part in spans], axis=0)
        for level in range(LEVELS):
            start = span + level * groups
            gquery = gquery + dot(grad_score[:, start : start + groups], far[level, head, :groups, :])
        here = pl.ds(head, tokens, stride=heads)
        gq_rows[here, :] = gquery
        gk_rows[here, :] = jnp.concatenate(
            [dot(grad_score[part, :span], query[part], TN) for part in spans], axis=0
        )
        gv_rows[here, :] = jnp.concatenate(
            [dot(rounded[part, :span], grad[part], TN) for part in spans], axis=0
        )
        normed_rows[here, :] = direction * gain

        @pl.when(head == 0)
        def _():
            loop(heads, gain_terms)

        for step in range(len(gain_ring) + 1):

            @pl.when(head == step)
            def _():
                gain_step(step)

        @pl.when(head >= lag)
        def _():
            join(head - lag)

    loop(heads, backward)

    def gather(rows, ref):
        def body(step):
            part = rows[pl.ds(pl.multiple_of(step * slab * heads, 8), slab * heads), :]
            ref[pl.ds(step * slab, slab)] = part.reshape(slab, heads, width).astype(jnp.bfloat16)

        loop(tokens // slab, body)

    for step in range(heads, len(gain_ring) + 1):
        gain_step(step)
    ggain_ref[...] = gain_out[len(gain_ring)]
    loop(lag, lambda step: join(heads - lag + step))
    gather(normed_rows, normed_ref)
    gather(gq_rows, gquery_ref)

    def collect(head):
        for kind in (B0, B2, B3):
            transfer(kind, head).wait_recv()
        total = (
            grad_in[0, head].astype(jnp.float32)
            + grad_in[2, head].astype(jnp.float32)
            + grad_in[3, head].astype(jnp.float32)
        )
        here = pl.ds(head, groups, stride=heads)
        ck_rows[here, :] = total[:groups] * (1.0 / COARSE)
        cv_rows[here, :] = total[groups:] * (1.0 / COARSE)

    loop(heads, collect)

    def merge(rows, coarse_rows, ref):
        def body(step):
            part = rows[pl.ds(pl.multiple_of(step * slab * heads, 8), slab * heads), :]
            half = slab // 2 * heads
            coarse = coarse_rows[pl.ds(pl.multiple_of(step * half, 8), half), :]
            whole = part.reshape(slab // 2, 2, heads, width) + coarse.reshape(
                slab // 2, 1, heads, width
            )
            ref[pl.ds(step * slab, slab)] = whole.reshape(slab, heads, width).astype(jnp.bfloat16)

        loop(tokens // slab, body)

    merge(gk_rows, ck_rows, gkeys_ref)
    merge(gv_rows, cv_rows, gvalues_ref)

    def drain(head):
        for kind in range(8):
            transfer(kind, head).wait_send()

    loop(heads, drain)
    for step in range(len(gain_ring)):
        gain_copy(step).wait_send()


def store(*refs):
    sources, targets, sems = refs[:5], refs[5:10], refs[10]
    copies = [
        pltpu.make_async_copy(source, target, sems.at[number])
        for number, (source, target) in enumerate(zip(sources, targets))
    ]
    for copy in copies:
        copy.start()
    for copy in copies:
        copy.wait()


def local(n_seq, query, keys, values, cotangent, gain):
    tokens, heads, width = query.shape
    groups = tokens // COARSE
    steps = n_seq.bit_length() - 1
    columns = 2 * BLOCK + LEVELS * groups
    whole = jax.ShapeDtypeStruct(query.shape, jnp.bfloat16)
    vmem = pl.BlockSpec(memory_space=pltpu.VMEM)
    hbm = pl.BlockSpec(memory_space=pltpu.HBM)
    block = pltpu.VMEM(query.shape, jnp.bfloat16)
    rows = pltpu.VMEM((tokens * heads, width), jnp.float32)
    coarse_rows = pltpu.VMEM((groups * heads, width), jnp.float32)
    wide = pltpu.VMEM((tokens, width), jnp.float32)
    pairs = (heads, 2 * groups, width)
    results = pl.pallas_call(
        functools.partial(kernel, n_seq),
        out_shape=[whole] * 4 + [jax.ShapeDtypeStruct(gain.shape, jnp.float32)],
        in_specs=[hbm] * 5,
        out_specs=[vmem] * 5,
        scratch_shapes=[
            block, block, block, block,
            pltpu.VMEM(gain.shape, jnp.float32),
            pltpu.SemaphoreType.DMA((5,)),
            rows, rows, rows, rows, coarse_rows, coarse_rows,
            pltpu.VMEM(pairs, jnp.bfloat16),
            pltpu.VMEM((LEVELS,) + pairs, jnp.bfloat16),
            pltpu.VMEM((heads, tokens, columns), jnp.float32),
            pltpu.VMEM((heads, tokens, width), jnp.float32),
            wide, wide,
            pltpu.VMEM((8, tokens), jnp.float32),
            pltpu.VMEM((8, tokens), jnp.float32),
            wide, wide,
            pltpu.VMEM((LEVELS,) + pairs, jnp.bfloat16),
            pltpu.VMEM((LEVELS,) + pairs, jnp.bfloat16),
            pltpu.VMEM(pairs, jnp.float32),
            pltpu.VMEM((steps + 1,) + gain.shape, jnp.float32),
            pltpu.VMEM((steps,) + gain.shape, jnp.float32),
            rows, rows, rows, rows,
            pltpu.SemaphoreType.DMA((8, heads)),
            pltpu.SemaphoreType.DMA((8, heads)),
            pltpu.SemaphoreType.DMA((2,)),
            pltpu.SemaphoreType.DMA((steps,)),
            pltpu.SemaphoreType.DMA((steps,)),
        ],
        compiler_params=pltpu.CompilerParams(
            collective_id=0, has_side_effects=True, vmem_limit_bytes=56 * 2**20
        ),
        cost_estimate=pl.CostEstimate(
            flops=1_800_000_000, bytes_accessed=4 * 2**20, transcendentals=1_200_000
        ),
    )(query, keys, values, cotangent, gain)
    return pl.pallas_call(
        store,
        out_shape=[jax.ShapeDtypeStruct(result.shape, result.dtype) for result in results],
        in_specs=[vmem] * 5,
        out_specs=[hbm] * 5,
        scratch_shapes=[pltpu.SemaphoreType.DMA((5,))],
    )(*results)


def solution(mesh):
    spec = P("seq", "head", None)
    return jax.shard_map(
        functools.partial(local, mesh.shape["seq"]),
        mesh=mesh,
        in_specs=(spec, spec, spec, spec, P("head", None)),
        out_specs=(spec, spec, spec, spec, P("head", None)),
        check_vma=False,
    )
```

```python
import functools

import jax
import jax.numpy as jnp
from jax import lax
from jax.experimental import pallas as pl
from jax.experimental.pallas import tpu as pltpu
from jax.sharding import PartitionSpec as P

HEADS = 16
HEAD_DIM = 128
BLOCK = 64
COARSE = 2
LEVELS = 4
EPSILON = 1e-05
MESH = pl.DeviceIdType.MESH
NT = (((1,), (1,)), ((), ()))
TN = (((0,), (0,)), ((), ()))

F0, F1, F2, F3, B0, B1, B2, B3 = range(8)


def flipped(index, distance):
    return index + distance - 2 * distance * ((index // distance) % 2)


def dot(left, right, dims=(((1,), (0,)), ((), ()))):
    return lax.dot_general(left, right, dims, preferred_element_type=jnp.float32)


def kernel(
    n_seq, query_hbm, keys_hbm, values_hbm, cotan_hbm, gain_hbm,
    normed_ref, gquery_ref, gkeys_ref, gvalues_ref, ggain_ref,
    query_ref, keys_ref, values_ref, cotan_ref, gain_ref, load_sems,
    q_rows, k_rows, v_rows, c_rows, ck_rows, cv_rows,
    own, far, probs, attn, sq_sum, slope_sum, norm_out, norm_in, inv_wide, coef_wide,
    grad_out, grad_in, level2, gain_out, gain_in,
    normed_rows, gq_rows, gk_rows, gv_rows,
    send_sem, recv_sem, norm_sems, gain_send, gain_recv,
):
    loads = [
        pltpu.make_async_copy(source, target, load_sems.at[number])
        for number, (source, target) in enumerate(
            [
                (keys_hbm, keys_ref),
                (values_hbm, values_ref),
                (query_hbm, query_ref),
                (cotan_hbm, cotan_ref),
                (gain_hbm, gain_ref),
            ]
        )
    ]
    for load in loads:
        load.start()
    tokens, heads, width = query_ref.shape
    groups = tokens // COARSE
    scale = width ** (-0.5)
    me = lax.axis_index("seq")
    side = lax.axis_index("head")
    distances = [n_seq >> level + 1 for level in range(LEVELS)]
    at0, at2, at3 = (flipped(me, distances[level]) for level in (0, 2, 3))
    relay = flipped(at2, distances[1])
    low = []
    while 1 << len(low) < distances[3]:
        low.append(flipped(me, 1 << len(low)))
    ring = low + [at3, at2, relay, at0]

    barrier = pltpu.get_barrier_semaphore()
    for partner in ring:
        pl.semaphore_signal(barrier, inc=1, device_id={"seq": partner}, device_id_type=MESH)
    pl.semaphore_signal(barrier, inc=1, device_id={"head": 1 - side}, device_id_type=MESH)

    def transfer(kind, head):
        source, target, partner = {
            F0: (own, far.at[0], at0),
            F1: (far.at[2], far.at[1], relay),
            F2: (own, far.at[2], at2),
            F3: (own, far.at[3], at3),
            B0: (grad_out.at[0], grad_in.at[0], at0),
            B1: (grad_out.at[1], grad_in.at[1], relay),
            B2: (grad_out.at[2], grad_in.at[2], at2),
            B3: (grad_out.at[3], grad_in.at[3], at3),
        }[kind]
        return pltpu.make_async_remote_copy(
            src_ref=source.at[head],
            dst_ref=target.at[head],
            send_sem=send_sem.at[kind, head],
            recv_sem=recv_sem.at[kind, head],
            device_id={"seq": partner},
            device_id_type=MESH,
        )

    def loop(count, body):
        def run(step, carry):
            body(step)
            return carry

        lax.fori_loop(0, count, run, 0)

    slab = 16

    def spread(ref, rows):
        def body(step):
            part = ref[pl.ds(step * slab, slab)].astype(jnp.float32)
            rows[pl.ds(pl.multiple_of(step * slab * heads, 8), slab * heads), :] = part.reshape(
                slab * heads, width
            )

        loop(tokens // slab, body)

    def coarsen(ref, rows, coarse_rows):
        def body(step):
            part = ref[pl.ds(step * slab, slab)].astype(jnp.float32)
            rows[pl.ds(pl.multiple_of(step * slab * heads, 8), slab * heads), :] = part.reshape(
                slab * heads, width
            )
            pairs = part.reshape(slab // 2, 2, heads, width)
            mean = (pairs[:, 0] + pairs[:, 1]) * 0.5
            half = slab // 2 * heads
            coarse_rows[pl.ds(pl.multiple_of(step * half, 8), half), :] = mean.reshape(half, width)

        loop(tokens // slab, body)

    def pick(rows, head, count):
        return rows[pl.ds(head, count, stride=heads), :]

    loads[0].wait()
    coarsen(keys_ref, k_rows, ck_rows)
    loads[1].wait()
    coarsen(values_ref, v_rows, cv_rows)

    def pack(head):
        own[head, :groups, :] = pick(ck_rows, head, groups).astype(jnp.bfloat16)
        own[head, groups:, :] = pick(cv_rows, head, groups).astype(jnp.bfloat16)

    loop(heads, pack)
    pl.semaphore_wait(barrier, len(ring) + 1)

    def first(head):
        transfer(F2, head).start()
        transfer(F0, head).start()

    loop(heads, first)
    early = heads // 2
    loop(early, lambda head: transfer(F3, head).start())
    for load in loads[2:]:
        load.wait()
    spread(query_ref, q_rows)
    spread(cotan_ref, c_rows)
    sq_sum[...] = jnp.zeros_like(sq_sum)
    slope_sum[...] = jnp.zeros_like(slope_sum)

    def forward(head):
        transfer(F2, head).wait_recv()
        transfer(F1, head).start()

        @pl.when(head >= early)
        def _():
            transfer(F3, head).start()

    loop(heads, forward)

    span = 2 * BLOCK
    row_block = lax.broadcasted_iota(jnp.int32, (span, span), 0) < BLOCK
    col_block = lax.broadcasted_iota(jnp.int32, (span, span), 1) < BLOCK
    inside = row_block == col_block
    spans = [slice(start, start + span) for start in range(0, tokens, span)]

    def attend(head):
        transfer(F0, head).wait_recv()
        transfer(F1, head).wait_recv()
        transfer(F3, head).wait_recv()
        query = pick(q_rows, head, tokens).astype(jnp.bfloat16)
        key = pick(k_rows, head, tokens).astype(jnp.bfloat16)
        value = pick(v_rows, head, tokens).astype(jnp.bfloat16)
        near = [
            jnp.where(inside, dot(query[part], key[part], NT) * scale, -1e30) for part in spans
        ]
        scores = [jnp.concatenate(near, axis=0)] + [
            dot(query, far[level, head, :groups, :], NT) * scale for level in range(LEVELS)
        ]
        scores = jnp.concatenate(scores, axis=1)
        top = jnp.max(scores, axis=1, keepdims=True)
        weights = jnp.exp(scores - top)
        total = jnp.sum(weights, axis=1, keepdims=True)
        prob = weights * (1.0 / total)
        probs[head] = prob
        rounded = prob.astype(jnp.bfloat16)
        out = jnp.concatenate([dot(rounded[part, :span], value[part]) for part in spans], axis=0)
        for level in range(LEVELS):
            start = span + level * groups
            out = out + dot(rounded[:, start : start + groups], far[level, head, groups:, :])
        attn[head] = out
        weighted = pick(c_rows, head, tokens) * gain_ref[pl.ds(head, 1), :]
        sq_sum[...] += out * out
        slope_sum[...] += weighted * out

    loop(heads, attend)

    norm_out[...] = jnp.zeros_like(norm_out)
    norm_out[0:1, :] = jnp.sum(sq_sum[...].T, axis=0, keepdims=True)
    norm_out[1:2, :] = jnp.sum(slope_sum[...].T, axis=0, keepdims=True)
    norm_copy = pltpu.make_async_remote_copy(
        src_ref=norm_out,
        dst_ref=norm_in,
        send_sem=norm_sems.at[0],
        recv_sem=norm_sems.at[1],
        device_id={"head": 1 - side},
        device_id_type=MESH,
    )
    norm_copy.start()
    norm_copy.wait()
    squares = norm_out[0:1, :] + norm_in[0:1, :]
    slope = norm_out[1:2, :] + norm_in[1:2, :]
    inverse = lax.rsqrt(squares / (HEADS * HEAD_DIM) + EPSILON)
    coef = inverse * inverse * inverse * slope / (HEADS * HEAD_DIM)
    inv_wide[...] = jnp.broadcast_to(inverse, (width, tokens)).T
    coef_wide[...] = jnp.broadcast_to(coef, (width, tokens)).T

    def join(head):
        transfer(B1, head).wait_recv()
        grad_out[2, head] = (level2[head] + grad_in[1, head].astype(jnp.float32)).astype(
            jnp.bfloat16
        )
        transfer(B2, head).start()

    lag = 2
    gain_ring = [ring[3], at3, at2, relay] + ring[:3] + [at0]

    def gain_terms(head):
        direction = attn[head] * inv_wide[...]
        gain_out[0, pl.ds(head, 1), :] = jnp.sum(
            pick(c_rows, head, tokens) * direction, axis=0, keepdims=True
        )

    def gain_copy(step):
        return pltpu.make_async_remote_copy(
            src_ref=gain_out.at[step],
            dst_ref=gain_in.at[step],
            send_sem=gain_send.at[step],
            recv_sem=gain_recv.at[step],
            device_id={"seq": gain_ring[step]},
            device_id_type=MESH,
        )

    def gain_step(step):
        if step:
            gain_copy(step - 1).wait_recv()
            gain_out[step] = gain_out[step - 1] + gain_in[step - 1]
        if step < len(gain_ring):
            gain_copy(step).start()

    def backward(head):
        query = pick(q_rows, head, tokens).astype(jnp.bfloat16)
        key = pick(k_rows, head, tokens).astype(jnp.bfloat16)
        value = pick(v_rows, head, tokens).astype(jnp.bfloat16)
        out = attn[head]
        gain = gain_ref[pl.ds(head, 1), :]
        cotan = pick(c_rows, head, tokens)
        direction = out * inv_wide[...]
        grad_attn = cotan * gain * inv_wide[...] - out * coef_wide[...]
        grad = grad_attn.astype(jnp.bfloat16)
        prob = probs[head]
        rounded = prob.astype(jnp.bfloat16)
        grad_prob = [
            jnp.concatenate([dot(grad[part], value[part], NT) for part in spans], axis=0)
        ] + [dot(grad, far[level, head, groups:, :], NT) for level in range(LEVELS)]
        grad_prob = jnp.concatenate(grad_prob, axis=1)
        correction = jnp.sum(grad_prob * prob, axis=1, keepdims=True)
        grad_score = (prob * (grad_prob - correction) * scale).astype(jnp.bfloat16)
        for level in (1, 0, 3, 2):
            start = span + level * groups
            dkey = dot(grad_score[:, start : start + groups], query, TN)
            dvalue = dot(rounded[:, start : start + groups], grad, TN)
            if level == 2:
                level2[head, :groups, :] = dkey
                level2[head, groups:, :] = dvalue
            else:
                grad_out[level, head, :groups, :] = dkey.astype(jnp.bfloat16)
                grad_out[level, head, groups:, :] = dvalue.astype(jnp.bfloat16)
            if level == 1:
                transfer(B1, head).start()
            elif level == 0:
                transfer(B0, head).start()
            elif level == 3:
                transfer(B3, head).start()

        gquery = jnp.concatenate([dot(grad_score[part, :span], key[part]) for part in spans], axis=0)
        for level in range(LEVELS):
            start = span + level * groups
            gquery = gquery + dot(grad_score[:, start : start + groups], far[level, head, :groups, :])
        here = pl.ds(head, tokens, stride=heads)
        gq_rows[here, :] = gquery
        gk_rows[here, :] = jnp.concatenate(
            [dot(grad_score[part, :span], query[part], TN) for part in spans], axis=0
        )
        gv_rows[here, :] = jnp.concatenate(
            [dot(rounded[part, :span], grad[part], TN) for part in spans], axis=0
        )
        normed_rows[here, :] = direction * gain

        @pl.when(head == 0)
        def _():
            loop(heads, gain_terms)

        for step in range(len(gain_ring) + 1):

            @pl.when(head == step)
            def _():
                gain_step(step)

        @pl.when(head >= lag)
        def _():
            join(head - lag)

    loop(heads, backward)

    def gather(rows, ref):
        def body(step):
            part = rows[pl.ds(pl.multiple_of(step * slab * heads, 8), slab * heads), :]
            ref[pl.ds(step * slab, slab)] = part.reshape(slab, heads, width).astype(jnp.bfloat16)

        loop(tokens // slab, body)

    for step in range(heads, len(gain_ring) + 1):
        gain_step(step)
    ggain_ref[...] = gain_out[len(gain_ring)]
    loop(lag, lambda step: join(heads - lag + step))
    gather(normed_rows, normed_ref)
    gather(gq_rows, gquery_ref)

    def collect(head):
        for kind in (B0, B2, B3):
            transfer(kind, head).wait_recv()
        total = (
            grad_in[0, head].astype(jnp.float32)
            + grad_in[2, head].astype(jnp.float32)
            + grad_in[3, head].astype(jnp.float32)
        )
        here = pl.ds(head, groups, stride=heads)
        ck_rows[here, :] = total[:groups] * (1.0 / COARSE)
        cv_rows[here, :] = total[groups:] * (1.0 / COARSE)

    loop(heads, collect)

    def merge(rows, coarse_rows, ref):
        def body(step):
            part = rows[pl.ds(pl.multiple_of(step * slab * heads, 8), slab * heads), :]
            half = slab // 2 * heads
            coarse = coarse_rows[pl.ds(pl.multiple_of(step * half, 8), half), :]
            whole = part.reshape(slab // 2, 2, heads, width) + coarse.reshape(
                slab // 2, 1, heads, width
            )
            ref[pl.ds(step * slab, slab)] = whole.reshape(slab, heads, width).astype(jnp.bfloat16)

        loop(tokens // slab, body)

    merge(gk_rows, ck_rows, gkeys_ref)
    merge(gv_rows, cv_rows, gvalues_ref)

    def drain(head):
        for kind in range(8):
            transfer(kind, head).wait_send()

    loop(heads, drain)
    for step in range(len(gain_ring)):
        gain_copy(step).wait_send()


def store(*refs):
    sources, targets, sems = refs[:5], refs[5:10], refs[10]
    copies = [
        pltpu.make_async_copy(source, target, sems.at[number])
        for number, (source, target) in enumerate(zip(sources, targets))
    ]
    for copy in copies:
        copy.start()
    for copy in copies:
        copy.wait()


def local(n_seq, query, keys, values, cotangent, gain):
    tokens, heads, width = query.shape
    groups = tokens // COARSE
    steps = n_seq.bit_length() - 1
    columns = 2 * BLOCK + LEVELS * groups
    whole = jax.ShapeDtypeStruct(query.shape, jnp.bfloat16)
    vmem = pl.BlockSpec(memory_space=pltpu.VMEM)
    hbm = pl.BlockSpec(memory_space=pltpu.HBM)
    block = pltpu.VMEM(query.shape, jnp.bfloat16)
    rows = pltpu.VMEM((tokens * heads, width), jnp.float32)
    coarse_rows = pltpu.VMEM((groups * heads, width), jnp.float32)
    wide = pltpu.VMEM((tokens, width), jnp.float32)
    pairs = (heads, 2 * groups, width)
    results = pl.pallas_call(
        functools.partial(kernel, n_seq),
        out_shape=[whole] * 4 + [jax.ShapeDtypeStruct(gain.shape, jnp.float32)],
        in_specs=[hbm] * 5,
        out_specs=[vmem] * 5,
        scratch_shapes=[
            block, block, block, block,
            pltpu.VMEM(gain.shape, jnp.float32),
            pltpu.SemaphoreType.DMA((5,)),
            rows, rows, rows, rows, coarse_rows, coarse_rows,
            pltpu.VMEM(pairs, jnp.bfloat16),
            pltpu.VMEM((LEVELS,) + pairs, jnp.bfloat16),
            pltpu.VMEM((heads, tokens, columns), jnp.float32),
            pltpu.VMEM((heads, tokens, width), jnp.float32),
            wide, wide,
            pltpu.VMEM((8, tokens), jnp.float32),
            pltpu.VMEM((8, tokens), jnp.float32),
            wide, wide,
            pltpu.VMEM((LEVELS,) + pairs, jnp.bfloat16),
            pltpu.VMEM((LEVELS,) + pairs, jnp.bfloat16),
            pltpu.VMEM(pairs, jnp.float32),
            pltpu.VMEM((steps + 1,) + gain.shape, jnp.float32),
            pltpu.VMEM((steps,) + gain.shape, jnp.float32),
            rows, rows, rows, rows,
            pltpu.SemaphoreType.DMA((8, heads)),
            pltpu.SemaphoreType.DMA((8, heads)),
            pltpu.SemaphoreType.DMA((2,)),
            pltpu.SemaphoreType.DMA((steps,)),
            pltpu.SemaphoreType.DMA((steps,)),
        ],
        compiler_params=pltpu.CompilerParams(
            collective_id=0, has_side_effects=True, vmem_limit_bytes=53120 * 1024
        ),
        cost_estimate=pl.CostEstimate(
            flops=1_800_000_000, bytes_accessed=4 * 2**20, transcendentals=1_200_000
        ),
    )(query, keys, values, cotangent, gain)
    return pl.pallas_call(
        store,
        out_shape=[jax.ShapeDtypeStruct(result.shape, result.dtype) for result in results],
        in_specs=[vmem] * 5,
        out_specs=[hbm] * 5,
        scratch_shapes=[pltpu.SemaphoreType.DMA((5,))],
        compiler_params=pltpu.CompilerParams(vmem_limit_bytes=2**20),
    )(*results)


def solution(mesh):
    spec = P("seq", "head", None)
    return jax.shard_map(
        functools.partial(local, mesh.shape["seq"]),
        mesh=mesh,
        in_specs=(spec, spec, spec, spec, P("head", None)),
        out_specs=(spec, spec, spec, spec, P("head", None)),
        check_vma=False,
    )
```

```python
import functools

import jax
import jax.numpy as jnp
from jax import lax
from jax.experimental import pallas as pl
from jax.experimental.pallas import tpu as pltpu
from jax.sharding import PartitionSpec as P

HEADS = 16
HEAD_DIM = 128
BLOCK = 64
COARSE = 2
LEVELS = 4
EPSILON = 1e-05
MESH = pl.DeviceIdType.MESH
NT = (((1,), (1,)), ((), ()))
TN = (((0,), (0,)), ((), ()))

F0, F1, F2, F3, B0, B1, B2, B3 = range(8)


def flipped(index, distance):
    return index + distance - 2 * distance * ((index // distance) % 2)


def dot(left, right, dims=(((1,), (0,)), ((), ()))):
    return lax.dot_general(left, right, dims, preferred_element_type=jnp.float32)


def kernel(
    n_seq, query_hbm, keys_hbm, values_hbm, cotan_hbm, gain_hbm,
    normed_ref, gquery_ref, gkeys_ref, gvalues_ref, ggain_ref,
    query_ref, keys_ref, values_ref, cotan_ref, gain_ref, load_sems,
    q_rows, k_rows, v_rows, c_rows, ck_rows, cv_rows,
    own, far, probs, attn, sq_sum, slope_sum, norm_out, norm_in, inv_wide, coef_wide,
    grad_out, grad_in, level2, gain_out, gain_in,
    normed_rows, gq_rows, gk_rows, gv_rows,
    send_sem, recv_sem, norm_sems, gain_send, gain_recv,
):
    loads = [
        pltpu.make_async_copy(source, target, load_sems.at[number])
        for number, (source, target) in enumerate(
            [
                (keys_hbm, keys_ref),
                (values_hbm, values_ref),
                (query_hbm, query_ref),
                (cotan_hbm, cotan_ref),
                (gain_hbm, gain_ref),
            ]
        )
    ]
    for load in loads:
        load.start()
    tokens, heads, width = query_ref.shape
    groups = tokens // COARSE
    scale = width ** (-0.5)
    me = lax.axis_index("seq")
    side = lax.axis_index("head")
    distances = [n_seq >> level + 1 for level in range(LEVELS)]
    at0, at2, at3 = (flipped(me, distances[level]) for level in (0, 2, 3))
    relay = flipped(at2, distances[1])
    low = []
    while 1 << len(low) < distances[3]:
        low.append(flipped(me, 1 << len(low)))
    ring = low + [at3, at2, relay, at0]

    barrier = pltpu.get_barrier_semaphore()
    for partner in ring:
        pl.semaphore_signal(barrier, inc=1, device_id={"seq": partner}, device_id_type=MESH)
    pl.semaphore_signal(barrier, inc=1, device_id={"head": 1 - side}, device_id_type=MESH)

    def transfer(kind, head):
        source, target, partner = {
            F0: (own, far.at[0], at0),
            F1: (far.at[2], far.at[1], relay),
            F2: (own, far.at[2], at2),
            F3: (own, far.at[3], at3),
            B0: (grad_out.at[0], grad_in.at[0], at0),
            B1: (grad_out.at[1], grad_in.at[1], relay),
            B2: (grad_out.at[2], grad_in.at[2], at2),
            B3: (grad_out.at[3], grad_in.at[3], at3),
        }[kind]
        return pltpu.make_async_remote_copy(
            src_ref=source.at[head],
            dst_ref=target.at[head],
            send_sem=send_sem.at[kind, head],
            recv_sem=recv_sem.at[kind, head],
            device_id={"seq": partner},
            device_id_type=MESH,
        )

    def loop(count, body):
        def run(step, carry):
            body(step)
            return carry

        lax.fori_loop(0, count, run, 0)

    slab = 16

    def spread(ref, rows):
        def body(step):
            part = ref[pl.ds(step * slab, slab)].astype(jnp.float32)
            rows[pl.ds(pl.multiple_of(step * slab * heads, 8), slab * heads), :] = part.reshape(
                slab * heads, width
            )

        loop(tokens // slab, body)

    def coarsen(ref, rows, coarse_rows):
        def body(step):
            part = ref[pl.ds(step * slab, slab)].astype(jnp.float32)
            rows[pl.ds(pl.multiple_of(step * slab * heads, 8), slab * heads), :] = part.reshape(
                slab * heads, width
            )
            pairs = part.reshape(slab // 2, 2, heads, width)
            mean = (pairs[:, 0] + pairs[:, 1]) * 0.5
            half = slab // 2 * heads
            coarse_rows[pl.ds(pl.multiple_of(step * half, 8), half), :] = mean.reshape(half, width)

        loop(tokens // slab, body)

    def pick(rows, head, count):
        return rows[pl.ds(head, count, stride=heads), :]

    loads[0].wait()
    coarsen(keys_ref, k_rows, ck_rows)
    loads[1].wait()
    coarsen(values_ref, v_rows, cv_rows)

    def pack(head):
        own[head, :groups, :] = pick(ck_rows, head, groups).astype(jnp.bfloat16)
        own[head, groups:, :] = pick(cv_rows, head, groups).astype(jnp.bfloat16)

    loop(heads, pack)
    pl.semaphore_wait(barrier, len(ring) + 1)

    def first(head):
        transfer(F2, head).start()
        transfer(F0, head).start()

    loop(heads, first)
    early = heads // 2
    loop(early, lambda head: transfer(F3, head).start())
    for load in loads[2:]:
        load.wait()
    spread(query_ref, q_rows)
    spread(cotan_ref, c_rows)
    sq_sum[...] = jnp.zeros_like(sq_sum)
    slope_sum[...] = jnp.zeros_like(slope_sum)

    def forward(head):
        transfer(F2, head).wait_recv()
        transfer(F1, head).start()

        @pl.when(head >= early)
        def _():
            transfer(F3, head).start()

    loop(heads, forward)

    span = 2 * BLOCK
    row_block = lax.broadcasted_iota(jnp.int32, (span, span), 0) < BLOCK
    col_block = lax.broadcasted_iota(jnp.int32, (span, span), 1) < BLOCK
    inside = row_block == col_block
    spans = [slice(start, start + span) for start in range(0, tokens, span)]

    def attend(head):
        transfer(F0, head).wait_recv()
        transfer(F1, head).wait_recv()
        transfer(F3, head).wait_recv()
        query = pick(q_rows, head, tokens).astype(jnp.bfloat16)
        key = pick(k_rows, head, tokens).astype(jnp.bfloat16)
        value = pick(v_rows, head, tokens).astype(jnp.bfloat16)
        near = [
            jnp.where(inside, dot(query[part], key[part], NT) * scale, -1e30) for part in spans
        ]
        scores = [jnp.concatenate(near, axis=0)] + [
            dot(query, far[level, head, :groups, :], NT) * scale for level in range(LEVELS)
        ]
        scores = jnp.concatenate(scores, axis=1)
        top = jnp.max(scores, axis=1, keepdims=True)
        weights = jnp.exp(scores - top)
        total = jnp.sum(weights, axis=1, keepdims=True)
        prob = weights * (1.0 / total)
        probs[head] = prob
        rounded = prob.astype(jnp.bfloat16)
        out = jnp.concatenate([dot(rounded[part, :span], value[part]) for part in spans], axis=0)
        for level in range(LEVELS):
            start = span + level * groups
            out = out + dot(rounded[:, start : start + groups], far[level, head, groups:, :])
        attn[head] = out
        weighted = pick(c_rows, head, tokens) * gain_ref[pl.ds(head, 1), :]
        sq_sum[...] += out * out
        slope_sum[...] += weighted * out

    loop(heads, attend)

    norm_out[...] = jnp.zeros_like(norm_out)
    norm_out[0:1, :] = jnp.sum(sq_sum[...].T, axis=0, keepdims=True)
    norm_out[1:2, :] = jnp.sum(slope_sum[...].T, axis=0, keepdims=True)
    norm_copy = pltpu.make_async_remote_copy(
        src_ref=norm_out,
        dst_ref=norm_in,
        send_sem=norm_sems.at[0],
        recv_sem=norm_sems.at[1],
        device_id={"head": 1 - side},
        device_id_type=MESH,
    )
    norm_copy.start()
    norm_copy.wait()
    squares = norm_out[0:1, :] + norm_in[0:1, :]
    slope = norm_out[1:2, :] + norm_in[1:2, :]
    inverse = lax.rsqrt(squares / (HEADS * HEAD_DIM) + EPSILON)
    coef = inverse * inverse * inverse * slope / (HEADS * HEAD_DIM)
    inv_wide[...] = jnp.broadcast_to(inverse, (width, tokens)).T
    coef_wide[...] = jnp.broadcast_to(coef, (width, tokens)).T

    def join(head):
        transfer(B1, head).wait_recv()
        grad_out[2, head] = (level2[head] + grad_in[1, head].astype(jnp.float32)).astype(
            jnp.bfloat16
        )
        transfer(B2, head).start()

    lag = 3
    gain_ring = [ring[3], at3, at2, relay] + ring[:3] + [at0]

    def gain_terms(head):
        direction = attn[head] * inv_wide[...]
        gain_out[0, pl.ds(head, 1), :] = jnp.sum(
            pick(c_rows, head, tokens) * direction, axis=0, keepdims=True
        )

    def gain_copy(step):
        return pltpu.make_async_remote_copy(
            src_ref=gain_out.at[step],
            dst_ref=gain_in.at[step],
            send_sem=gain_send.at[step],
            recv_sem=gain_recv.at[step],
            device_id={"seq": gain_ring[step]},
            device_id_type=MESH,
        )

    def gain_step(step):
        if step:
            gain_copy(step - 1).wait_recv()
            gain_out[step] = gain_out[step - 1] + gain_in[step - 1]
        if step < len(gain_ring):
            gain_copy(step).start()

    def backward(head):
        query = pick(q_rows, head, tokens).astype(jnp.bfloat16)
        key = pick(k_rows, head, tokens).astype(jnp.bfloat16)
        value = pick(v_rows, head, tokens).astype(jnp.bfloat16)
        out = attn[head]
        gain = gain_ref[pl.ds(head, 1), :]
        cotan = pick(c_rows, head, tokens)
        direction = out * inv_wide[...]
        grad_attn = cotan * gain * inv_wide[...] - out * coef_wide[...]
        grad = grad_attn.astype(jnp.bfloat16)
        prob = probs[head]
        rounded = prob.astype(jnp.bfloat16)
        grad_prob = [
            jnp.concatenate([dot(grad[part], value[part], NT) for part in spans], axis=0)
        ] + [dot(grad, far[level, head, groups:, :], NT) for level in range(LEVELS)]
        grad_prob = jnp.concatenate(grad_prob, axis=1)
        correction = jnp.sum(grad_prob * prob, axis=1, keepdims=True)
        grad_score = (prob * (grad_prob - correction) * scale).astype(jnp.bfloat16)
        for level in (1, 3, 0, 2):
            start = span + level * groups
            dkey = dot(grad_score[:, start : start + groups], query, TN)
            dvalue = dot(rounded[:, start : start + groups], grad, TN)
            if level == 2:
                level2[head, :groups, :] = dkey
                level2[head, groups:, :] = dvalue
            else:
                grad_out[level, head, :groups, :] = dkey.astype(jnp.bfloat16)
                grad_out[level, head, groups:, :] = dvalue.astype(jnp.bfloat16)
            if level == 1:
                transfer(B1, head).start()
            elif level == 0:
                transfer(B0, head).start()
            elif level == 3:
                transfer(B3, head).start()

        gquery = jnp.concatenate([dot(grad_score[part, :span], key[part]) for part in spans], axis=0)
        for level in range(LEVELS):
            start = span + level * groups
            gquery = gquery + dot(grad_score[:, start : start + groups], far[level, head, :groups, :])
        here = pl.ds(head, tokens, stride=heads)
        gq_rows[here, :] = gquery
        gk_rows[here, :] = jnp.concatenate(
            [dot(grad_score[part, :span], query[part], TN) for part in spans], axis=0
        )
        gv_rows[here, :] = jnp.concatenate(
            [dot(rounded[part, :span], grad[part], TN) for part in spans], axis=0
        )
        normed_rows[here, :] = direction * gain

        for step in range(1, len(gain_ring) + 1):

            @pl.when(head == step - 1)
            def _():
                gain_step(step)

        @pl.when(head >= lag)
        def _():
            join(head - lag)

    loop(heads, gain_terms)
    gain_step(0)
    loop(heads, backward)

    def gather(rows, ref):
        def body(step):
            part = rows[pl.ds(pl.multiple_of(step * slab * heads, 8), slab * heads), :]
            ref[pl.ds(step * slab, slab)] = part.reshape(slab, heads, width).astype(jnp.bfloat16)

        loop(tokens // slab, body)

    for step in range(heads + 1, len(gain_ring) + 1):
        gain_step(step)
    ggain_ref[...] = gain_out[len(gain_ring)]
    loop(lag, lambda step: join(heads - lag + step))
    gather(normed_rows, normed_ref)
    gather(gq_rows, gquery_ref)

    def collect(head):
        for kind in (B0, B2, B3):
            transfer(kind, head).wait_recv()
        total = (
            grad_in[0, head].astype(jnp.float32)
            + grad_in[2, head].astype(jnp.float32)
            + grad_in[3, head].astype(jnp.float32)
        )
        here = pl.ds(head, groups, stride=heads)
        ck_rows[here, :] = total[:groups] * (1.0 / COARSE)
        cv_rows[here, :] = total[groups:] * (1.0 / COARSE)

    loop(heads, collect)

    def merge(rows, coarse_rows, ref):
        def body(step):
            part = rows[pl.ds(pl.multiple_of(step * slab * heads, 8), slab * heads), :]
            half = slab // 2 * heads
            coarse = coarse_rows[pl.ds(pl.multiple_of(step * half, 8), half), :]
            whole = part.reshape(slab // 2, 2, heads, width) + coarse.reshape(
                slab // 2, 1, heads, width
            )
            ref[pl.ds(step * slab, slab)] = whole.reshape(slab, heads, width).astype(jnp.bfloat16)

        loop(tokens // slab, body)

    merge(gk_rows, ck_rows, gkeys_ref)
    merge(gv_rows, cv_rows, gvalues_ref)

    def drain(head):
        for kind in range(8):
            transfer(kind, head).wait_send()

    loop(heads, drain)
    for step in range(len(gain_ring)):
        gain_copy(step).wait_send()


def store(*refs):
    sources, targets, sems = refs[:5], refs[5:10], refs[10]
    copies = [
        pltpu.make_async_copy(source, target, sems.at[number])
        for number, (source, target) in enumerate(zip(sources, targets))
    ]
    for copy in copies:
        copy.start()
    for copy in copies:
        copy.wait()


def local(n_seq, query, keys, values, cotangent, gain):
    tokens, heads, width = query.shape
    groups = tokens // COARSE
    steps = n_seq.bit_length() - 1
    columns = 2 * BLOCK + LEVELS * groups
    whole = jax.ShapeDtypeStruct(query.shape, jnp.bfloat16)
    vmem = pl.BlockSpec(memory_space=pltpu.VMEM)
    hbm = pl.BlockSpec(memory_space=pltpu.HBM)
    block = pltpu.VMEM(query.shape, jnp.bfloat16)
    rows = pltpu.VMEM((tokens * heads, width), jnp.float32)
    coarse_rows = pltpu.VMEM((groups * heads, width), jnp.float32)
    wide = pltpu.VMEM((tokens, width), jnp.float32)
    pairs = (heads, 2 * groups, width)
    results = pl.pallas_call(
        functools.partial(kernel, n_seq),
        out_shape=[whole] * 4 + [jax.ShapeDtypeStruct(gain.shape, jnp.float32)],
        in_specs=[hbm] * 5,
        out_specs=[vmem] * 5,
        scratch_shapes=[
            block, block, block, block,
            pltpu.VMEM(gain.shape, jnp.float32),
            pltpu.SemaphoreType.DMA((5,)),
            rows, rows, rows, rows, coarse_rows, coarse_rows,
            pltpu.VMEM(pairs, jnp.bfloat16),
            pltpu.VMEM((LEVELS,) + pairs, jnp.bfloat16),
            pltpu.VMEM((heads, tokens, columns), jnp.float32),
            pltpu.VMEM((heads, tokens, width), jnp.float32),
            wide, wide,
            pltpu.VMEM((8, tokens), jnp.float32),
            pltpu.VMEM((8, tokens), jnp.float32),
            wide, wide,
            pltpu.VMEM((LEVELS,) + pairs, jnp.bfloat16),
            pltpu.VMEM((LEVELS,) + pairs, jnp.bfloat16),
            pltpu.VMEM(pairs, jnp.float32),
            pltpu.VMEM((steps + 1,) + gain.shape, jnp.float32),
            pltpu.VMEM((steps,) + gain.shape, jnp.float32),
            rows, rows, rows, rows,
            pltpu.SemaphoreType.DMA((8, heads)),
            pltpu.SemaphoreType.DMA((8, heads)),
            pltpu.SemaphoreType.DMA((2,)),
            pltpu.SemaphoreType.DMA((steps,)),
            pltpu.SemaphoreType.DMA((steps,)),
        ],
        compiler_params=pltpu.CompilerParams(
            collective_id=0, has_side_effects=True, vmem_limit_bytes=53120 * 1024
        ),
        cost_estimate=pl.CostEstimate(
            flops=1_800_000_000, bytes_accessed=4 * 2**20, transcendentals=1_200_000
        ),
    )(query, keys, values, cotangent, gain)
    return pl.pallas_call(
        store,
        out_shape=[jax.ShapeDtypeStruct(result.shape, result.dtype) for result in results],
        in_specs=[vmem] * 5,
        out_specs=[hbm] * 5,
        scratch_shapes=[pltpu.SemaphoreType.DMA((5,))],
        compiler_params=pltpu.CompilerParams(vmem_limit_bytes=2**20),
    )(*results)


def solution(mesh):
    spec = P("seq", "head", None)
    return jax.shard_map(
        functools.partial(local, mesh.shape["seq"]),
        mesh=mesh,
        in_specs=(spec, spec, spec, spec, P("head", None)),
        out_specs=(spec, spec, spec, spec, P("head", None)),
        check_vma=False,
    )
```

```python
import functools

import jax
import jax.numpy as jnp
from jax import lax
from jax.experimental import pallas as pl
from jax.experimental.pallas import tpu as pltpu
from jax.sharding import PartitionSpec as P

HEADS = 16
HEAD_DIM = 128
BLOCK = 64
COARSE = 2
LEVELS = 4
EPSILON = 1e-05
MESH = pl.DeviceIdType.MESH
NT = (((1,), (1,)), ((), ()))
TN = (((0,), (0,)), ((), ()))

F0, F1, F2, F3, B0, B1, B2, B3 = range(8)


def flipped(index, distance):
    return index + distance - 2 * distance * ((index // distance) % 2)


def dot(left, right, dims=(((1,), (0,)), ((), ()))):
    return lax.dot_general(left, right, dims, preferred_element_type=jnp.float32)


def kernel(
    n_seq, query_hbm, keys_hbm, values_hbm, cotan_hbm, gain_hbm,
    normed_ref, gquery_ref, gkeys_ref, gvalues_ref, ggain_ref,
    query_ref, keys_ref, values_ref, cotan_ref, gain_ref, load_sems,
    q_rows, k_rows, v_rows, c_rows, ck_rows, cv_rows,
    own, far, probs, attn, sq_sum, slope_sum, norm_out, norm_in, inv_wide, coef_wide,
    grad_out, grad_in, level2, gain_out, gain_in,
    normed_rows, gq_rows, gk_rows, gv_rows,
    send_sem, recv_sem, norm_sems, gain_send, gain_recv,
):
    loads = [
        pltpu.make_async_copy(source, target, load_sems.at[number])
        for number, (source, target) in enumerate(
            [
                (keys_hbm, keys_ref),
                (values_hbm, values_ref),
                (query_hbm, query_ref),
                (cotan_hbm, cotan_ref),
                (gain_hbm, gain_ref),
            ]
        )
    ]
    for load in loads:
        load.start()
    tokens, heads, width = query_ref.shape
    groups = tokens // COARSE
    scale = width ** (-0.5)
    me = lax.axis_index("seq")
    side = lax.axis_index("head")
    distances = [n_seq >> level + 1 for level in range(LEVELS)]
    at0, at2, at3 = (flipped(me, distances[level]) for level in (0, 2, 3))
    relay = flipped(at2, distances[1])
    low = []
    while 1 << len(low) < distances[3]:
        low.append(flipped(me, 1 << len(low)))
    ring = low + [at3, at2, relay, at0]

    barrier = pltpu.get_barrier_semaphore()
    for partner in ring:
        pl.semaphore_signal(barrier, inc=1, device_id={"seq": partner}, device_id_type=MESH)
    pl.semaphore_signal(barrier, inc=1, device_id={"head": 1 - side}, device_id_type=MESH)

    def transfer(kind, head):
        source, target, partner = {
            F0: (own, far.at[0], at0),
            F1: (far.at[2], far.at[1], relay),
            F2: (own, far.at[2], at2),
            F3: (own, far.at[3], at3),
            B0: (grad_out.at[0], grad_in.at[0], at0),
            B1: (grad_out.at[1], grad_in.at[1], relay),
            B2: (grad_out.at[2], grad_in.at[2], at2),
            B3: (grad_out.at[3], grad_in.at[3], at3),
        }[kind]
        return pltpu.make_async_remote_copy(
            src_ref=source.at[head],
            dst_ref=target.at[head],
            send_sem=send_sem.at[kind, head],
            recv_sem=recv_sem.at[kind, head],
            device_id={"seq": partner},
            device_id_type=MESH,
        )

    def loop(count, body):
        def run(step, carry):
            body(step)
            return carry

        lax.fori_loop(0, count, run, 0)

    slab = 16

    def spread(ref, rows):
        def body(step):
            part = ref[pl.ds(step * slab, slab)].astype(jnp.float32)
            rows[pl.ds(pl.multiple_of(step * slab * heads, 8), slab * heads), :] = part.reshape(
                slab * heads, width
            )

        loop(tokens // slab, body)

    def coarsen(ref, rows, coarse_rows):
        def body(step):
            part = ref[pl.ds(step * slab, slab)].astype(jnp.float32)
            rows[pl.ds(pl.multiple_of(step * slab * heads, 8), slab * heads), :] = part.reshape(
                slab * heads, width
            )
            pairs = part.reshape(slab // 2, 2, heads, width)
            mean = (pairs[:, 0] + pairs[:, 1]) * 0.5
            half = slab // 2 * heads
            coarse_rows[pl.ds(pl.multiple_of(step * half, 8), half), :] = mean.reshape(half, width)

        loop(tokens // slab, body)

    def pick(rows, head, count):
        return rows[pl.ds(head, count, stride=heads), :]

    loads[0].wait()
    coarsen(keys_ref, k_rows, ck_rows)
    loads[1].wait()
    coarsen(values_ref, v_rows, cv_rows)

    def pack(head):
        own[head, :groups, :] = pick(ck_rows, head, groups).astype(jnp.bfloat16)
        own[head, groups:, :] = pick(cv_rows, head, groups).astype(jnp.bfloat16)

    loop(heads, pack)
    pl.semaphore_wait(barrier, len(ring) + 1)

    def first(head):
        transfer(F2, head).start()
        transfer(F0, head).start()

    loop(heads, first)
    early = heads // 2
    loop(early, lambda head: transfer(F3, head).start())
    for load in loads[2:]:
        load.wait()
    spread(query_ref, q_rows)
    spread(cotan_ref, c_rows)
    sq_sum[...] = jnp.zeros_like(sq_sum)
    slope_sum[...] = jnp.zeros_like(slope_sum)

    def forward(head):
        transfer(F2, head).wait_recv()
        transfer(F1, head).start()

        @pl.when(head >= early)
        def _():
            transfer(F3, head).start()

    loop(heads, forward)

    span = 2 * BLOCK
    row_block = lax.broadcasted_iota(jnp.int32, (span, span), 0) < BLOCK
    col_block = lax.broadcasted_iota(jnp.int32, (span, span), 1) < BLOCK
    inside = row_block == col_block
    spans = [slice(start, start + span) for start in range(0, tokens, span)]

    def attend(head):
        transfer(F0, head).wait_recv()
        transfer(F1, head).wait_recv()
        transfer(F3, head).wait_recv()
        query = pick(q_rows, head, tokens).astype(jnp.bfloat16)
        key = pick(k_rows, head, tokens).astype(jnp.bfloat16)
        value = pick(v_rows, head, tokens).astype(jnp.bfloat16)
        near = [
            jnp.where(inside, dot(query[part], key[part], NT) * scale, -1e30) for part in spans
        ]
        scores = [jnp.concatenate(near, axis=0)] + [
            dot(query, far[level, head, :groups, :], NT) * scale for level in range(LEVELS)
        ]
        scores = jnp.concatenate(scores, axis=1)
        top = jnp.max(scores, axis=1, keepdims=True)
        weights = jnp.exp(scores - top)
        total = jnp.sum(weights, axis=1, keepdims=True)
        prob = weights * (1.0 / total)
        probs[head] = prob
        rounded = prob.astype(jnp.bfloat16)
        out = jnp.concatenate([dot(rounded[part, :span], value[part]) for part in spans], axis=0)
        for level in range(LEVELS):
            start = span + level * groups
            out = out + dot(rounded[:, start : start + groups], far[level, head, groups:, :])
        attn[head] = out
        weighted = pick(c_rows, head, tokens) * gain_ref[pl.ds(head, 1), :]
        sq_sum[...] += out * out
        slope_sum[...] += weighted * out

    loop(heads, attend)

    norm_out[...] = jnp.zeros_like(norm_out)
    norm_out[0:1, :] = jnp.sum(sq_sum[...].T, axis=0, keepdims=True)
    norm_out[1:2, :] = jnp.sum(slope_sum[...].T, axis=0, keepdims=True)
    norm_copy = pltpu.make_async_remote_copy(
        src_ref=norm_out,
        dst_ref=norm_in,
        send_sem=norm_sems.at[0],
        recv_sem=norm_sems.at[1],
        device_id={"head": 1 - side},
        device_id_type=MESH,
    )
    norm_copy.start()
    norm_copy.wait()
    squares = norm_out[0:1, :] + norm_in[0:1, :]
    slope = norm_out[1:2, :] + norm_in[1:2, :]
    inverse = lax.rsqrt(squares / (HEADS * HEAD_DIM) + EPSILON)
    coef = inverse * inverse * inverse * slope / (HEADS * HEAD_DIM)
    inv_wide[...] = jnp.broadcast_to(inverse, (width, tokens)).T
    coef_wide[...] = jnp.broadcast_to(coef, (width, tokens)).T

    def join(head):
        transfer(B1, head).wait_recv()
        grad_out[2, head] = (level2[head] + grad_in[1, head].astype(jnp.float32)).astype(
            jnp.bfloat16
        )
        transfer(B2, head).start()

    lag = 3
    gain_ring = [ring[3], at3, at2, relay] + ring[:3] + [at0]

    def gain_terms(head):
        direction = attn[head] * inv_wide[...]
        gain_out[0, pl.ds(head, 1), :] = jnp.sum(
            pick(c_rows, head, tokens) * direction, axis=0, keepdims=True
        )

    def gain_copy(step):
        return pltpu.make_async_remote_copy(
            src_ref=gain_out.at[step],
            dst_ref=gain_in.at[step],
            send_sem=gain_send.at[step],
            recv_sem=gain_recv.at[step],
            device_id={"seq": gain_ring[step]},
            device_id_type=MESH,
        )

    def gain_step(step):
        if step:
            gain_copy(step - 1).wait_recv()
            gain_out[step] = gain_out[step - 1] + gain_in[step - 1]
        if step < len(gain_ring):
            gain_copy(step).start()

    def backward(head):
        query = pick(q_rows, head, tokens).astype(jnp.bfloat16)
        key = pick(k_rows, head, tokens).astype(jnp.bfloat16)
        value = pick(v_rows, head, tokens).astype(jnp.bfloat16)
        out = attn[head]
        gain = gain_ref[pl.ds(head, 1), :]
        cotan = pick(c_rows, head, tokens)
        direction = out * inv_wide[...]
        grad_attn = cotan * gain * inv_wide[...] - out * coef_wide[...]
        grad = grad_attn.astype(jnp.bfloat16)
        prob = probs[head]
        rounded = prob.astype(jnp.bfloat16)
        grad_prob = [
            jnp.concatenate([dot(grad[part], value[part], NT) for part in spans], axis=0)
        ] + [dot(grad, far[level, head, groups:, :], NT) for level in range(LEVELS)]
        grad_prob = jnp.concatenate(grad_prob, axis=1)
        correction = jnp.sum(grad_prob * prob, axis=1, keepdims=True)
        grad_score = (prob * (grad_prob - correction) * scale).astype(jnp.bfloat16)
        for level in (1, 3, 0, 2):
            start = span + level * groups
            dkey = dot(grad_score[:, start : start + groups], query, TN)
            dvalue = dot(rounded[:, start : start + groups], grad, TN)
            if level == 2:
                level2[head, :groups, :] = dkey
                level2[head, groups:, :] = dvalue
            else:
                grad_out[level, head, :groups, :] = dkey.astype(jnp.bfloat16)
                grad_out[level, head, groups:, :] = dvalue.astype(jnp.bfloat16)
            if level == 1:
                transfer(B1, head).start()
            elif level == 0:
                transfer(B0, head).start()
            elif level == 3:
                transfer(B3, head).start()

        gquery = jnp.concatenate([dot(grad_score[part, :span], key[part]) for part in spans], axis=0)
        for level in range(LEVELS):
            start = span + level * groups
            gquery = gquery + dot(grad_score[:, start : start + groups], far[level, head, :groups, :])
        here = pl.ds(head, tokens, stride=heads)
        gq_rows[here, :] = gquery
        gk_rows[here, :] = jnp.concatenate(
            [dot(grad_score[part, :span], query[part], TN) for part in spans], axis=0
        )
        gv_rows[here, :] = jnp.concatenate(
            [dot(rounded[part, :span], grad[part], TN) for part in spans], axis=0
        )
        normed_rows[here, :] = direction * gain

        for step in range(1, len(gain_ring) + 1):

            @pl.when(head == step - 1)
            def _():
                gain_step(step)

        @pl.when(head >= lag)
        def _():
            join(head - lag)

    loop(heads, gain_terms)
    gain_step(0)
    loop(heads, backward)

    def gather(rows, ref):
        def body(step):
            part = rows[pl.ds(pl.multiple_of(step * slab * heads, 8), slab * heads), :]
            ref[pl.ds(step * slab, slab)] = part.reshape(slab, heads, width).astype(jnp.bfloat16)

        loop(tokens // slab, body)

    for step in range(heads + 1, len(gain_ring) + 1):
        gain_step(step)
    ggain_ref[...] = gain_out[len(gain_ring)]
    loop(lag, lambda step: join(heads - lag + step))
    gather(normed_rows, normed_ref)
    gather(gq_rows, gquery_ref)

    def collect(head):
        for kind in (B0, B2, B3):
            transfer(kind, head).wait_recv()
        total = (
            grad_in[0, head].astype(jnp.float32)
            + grad_in[2, head].astype(jnp.float32)
            + grad_in[3, head].astype(jnp.float32)
        )
        here = pl.ds(head, groups, stride=heads)
        ck_rows[here, :] = total[:groups] * (1.0 / COARSE)
        cv_rows[here, :] = total[groups:] * (1.0 / COARSE)

    loop(heads, collect)

    def merge(rows, coarse_rows, ref):
        def body(step):
            part = rows[pl.ds(pl.multiple_of(step * slab * heads, 8), slab * heads), :]
            half = slab // 2 * heads
            coarse = coarse_rows[pl.ds(pl.multiple_of(step * half, 8), half), :]
            whole = part.reshape(slab // 2, 2, heads, width) + coarse.reshape(
                slab // 2, 1, heads, width
            )
            ref[pl.ds(step * slab, slab)] = whole.reshape(slab, heads, width).astype(jnp.bfloat16)

        loop(tokens // slab, body)

    merge(gk_rows, ck_rows, gkeys_ref)
    merge(gv_rows, cv_rows, gvalues_ref)

    def drain(head):
        for kind in range(8):
            transfer(kind, head).wait_send()

    loop(heads, drain)
    for step in range(len(gain_ring)):
        gain_copy(step).wait_send()


def store(*refs):
    sources, targets, sems = refs[:5], refs[5:10], refs[10]
    copies = [
        pltpu.make_async_copy(source, target, sems.at[number])
        for number, (source, target) in enumerate(zip(sources, targets))
    ]
    for copy in copies:
        copy.start()
    for copy in copies:
        copy.wait()


def local(n_seq, query, keys, values, cotangent, gain):
    tokens, heads, width = query.shape
    groups = tokens // COARSE
    steps = n_seq.bit_length() - 1
    columns = 2 * BLOCK + LEVELS * groups
    whole = jax.ShapeDtypeStruct(query.shape, jnp.bfloat16)
    vmem = pl.BlockSpec(memory_space=pltpu.VMEM)
    hbm = pl.BlockSpec(memory_space=pltpu.HBM)
    block = pltpu.VMEM(query.shape, jnp.bfloat16)
    rows = pltpu.VMEM((tokens * heads + heads, width), jnp.float32)
    coarse_rows = pltpu.VMEM((groups * heads + heads, width), jnp.float32)
    wide = pltpu.VMEM((tokens, width), jnp.float32)
    pairs = (heads, 2 * groups, width)
    results = pl.pallas_call(
        functools.partial(kernel, n_seq),
        out_shape=[whole] * 4 + [jax.ShapeDtypeStruct(gain.shape, jnp.float32)],
        in_specs=[hbm] * 5,
        out_specs=[vmem] * 5,
        scratch_shapes=[
            block, block, block, block,
            pltpu.VMEM(gain.shape, jnp.float32),
            pltpu.SemaphoreType.DMA((5,)),
            rows, rows, rows, rows, coarse_rows, coarse_rows,
            pltpu.VMEM(pairs, jnp.bfloat16),
            pltpu.VMEM((LEVELS,) + pairs, jnp.bfloat16),
            pltpu.VMEM((heads, tokens, columns), jnp.float32),
            pltpu.VMEM((heads, tokens, width), jnp.float32),
            wide, wide,
            pltpu.VMEM((8, tokens), jnp.float32),
            pltpu.VMEM((8, tokens), jnp.float32),
            wide, wide,
            pltpu.VMEM((LEVELS,) + pairs, jnp.bfloat16),
            pltpu.VMEM((LEVELS,) + pairs, jnp.bfloat16),
            pltpu.VMEM(pairs, jnp.float32),
            pltpu.VMEM((steps + 1,) + gain.shape, jnp.float32),
            pltpu.VMEM((steps,) + gain.shape, jnp.float32),
            rows, rows, rows, rows,
            pltpu.SemaphoreType.DMA((8, heads)),
            pltpu.SemaphoreType.DMA((8, heads)),
            pltpu.SemaphoreType.DMA((2,)),
            pltpu.SemaphoreType.DMA((steps,)),
            pltpu.SemaphoreType.DMA((steps,)),
        ],
        compiler_params=pltpu.CompilerParams(
            collective_id=0, has_side_effects=True, vmem_limit_bytes=53120 * 1024
        ),
        cost_estimate=pl.CostEstimate(
            flops=1_800_000_000, bytes_accessed=4 * 2**20, transcendentals=1_200_000
        ),
    )(query, keys, values, cotangent, gain)
    return pl.pallas_call(
        store,
        out_shape=[jax.ShapeDtypeStruct(result.shape, result.dtype) for result in results],
        in_specs=[vmem] * 5,
        out_specs=[hbm] * 5,
        scratch_shapes=[pltpu.SemaphoreType.DMA((5,))],
        compiler_params=pltpu.CompilerParams(vmem_limit_bytes=2**20),
    )(*results)


def solution(mesh):
    spec = P("seq", "head", None)
    return jax.shard_map(
        functools.partial(local, mesh.shape["seq"]),
        mesh=mesh,
        in_specs=(spec, spec, spec, spec, P("head", None)),
        out_specs=(spec, spec, spec, spec, P("head", None)),
        check_vma=False,
    )
```
